256 devices in a mesh: tm: 32 (over z_lo, x, core), mode: 8 (over z_hi, y).
Axes of the slice: x: 4, y: 4, z: 8 (z_hi: 2, z_lo: 4; z = z_hi * 4 + z_lo), core: 2. Of those that a mesh axis runs over, the one named last changes fastest.
Arguments:
- fields: float32 [32, 2, 1024, 1024], P('tm', None, 'mode'), may hold values from -2.5 to 2.5
- offsets: int32 [32, 2], P('tm'), may hold values from 1 to 4
Outputs:
- products: float32 [32, 2, 2, 1024, 1024], P('tm', None, None, 'mode')
- correlators: float32 [32, 2], P('tm')
The draws below stay inside these ranges and needn't reach their ends.
All inputs are finite; a program needn't handle non-finite values.
Results may differ from the reference program's by a relative error of at most 0.0003.
Values sent between devices are 32-bit elements; how exact they have to be, the bound alone decides.
A program may use at most 128 MiB of HBM per device.

```python
import jax
import jax.numpy as jnp
from jax import lax

N = 1024
K = 2
TS = 32


def place_ends(values, own_key, smallest, largest):
    shape = values.shape
    place = [jax.random.randint(jax.random.fold_in(own_key, axis), (), 0, shape[axis]) for axis in range(len(shape))]
    values = values.at[tuple(place)].set(smallest)
    longest = shape.index(max(shape))
    place[longest] = (place[longest] + 1) % shape[longest]
    return values.at[tuple(place)].set(largest)


def level_of(stream_key, dims, cuts, smallest, high):
    loudness = 1.0
    for dim, blocks in cuts:
        heights = jax.random.uniform(jax.random.fold_in(jax.random.fold_in(stream_key, 6), dim), (blocks,), jnp.float32, smallest / len(cuts), high / len(cuts))
        loudness = loudness * jnp.repeat(jnp.exp(heights), dims[dim] // blocks).reshape((-1,) + (1,) * (len(dims) - 1 - dim))
    return loudness


def normal_values(own_key, shape, spread, limit, pieces=(), kind=jnp.bfloat16):
    entries = spread * jax.random.normal(own_key, shape, jnp.float32)
    if pieces:
        entries = entries * level_of(own_key, shape, pieces, -0.22, 0.18)
    return jnp.clip(entries, -limit, limit).astype(kind)


def setup_inputs(seed: int = 0) -> dict:
    key_list = jax.random.split(jax.random.key(seed), 3)
    fields = normal_values(key_list[0], (TS, 2, N, N), (N ** -0.25), 2.5, ((0, 32), (2, 8)), jnp.float32)
    offsets = place_ends(jax.random.randint(key_list[1], (TS, K), 1, 5), jax.random.fold_in(key_list[1], 1), 1, 4).astype(jnp.int32)
    return dict(fields=fields, offsets=offsets)


def complex_product(left, right):
    hi = lax.Precision.HIGHEST
    real = jnp.dot(left[0], right[0], precision=hi, preferred_element_type=jnp.float32) - jnp.dot(left[1], right[1], precision=hi, preferred_element_type=jnp.float32)
    imag = jnp.dot(left[0], right[1], precision=hi, preferred_element_type=jnp.float32) + jnp.dot(left[1], right[0], precision=hi, preferred_element_type=jnp.float32)
    return jnp.stack([real, imag])


def reference(fields, offsets):
    count = fields.shape[0]
    width = fields.shape[2]

    def one_pair(item):
        source = item[0]
        offset = item[1]
        sink = (source + offset) % count
        left = lax.dynamic_index_in_dim(fields, source.astype(jnp.int32), 0, keepdims=False)
        right = lax.dynamic_index_in_dim(fields, sink.astype(jnp.int32), 0, keepdims=False)
        forward = complex_product(left, right)
        partner = complex_product(right, left)
        trace = jnp.sum(forward * partner) / jnp.float32(width)
        return forward, trace

    sources = jnp.repeat(jnp.arange(count, dtype=jnp.int32), offsets.shape[1])
    items = jnp.stack([sources, offsets.reshape(-1).astype(jnp.int32)], axis=1)
    forward, trace = lax.map(one_pair, items)
    products = forward.reshape((count, offsets.shape[1]) + forward.shape[1:])
    correlators = trace.reshape(count, offsets.shape[1])
    return products, correlators
```

```python
import functools

import jax
import jax.numpy as jnp
from jax import lax
from jax.experimental import pallas as pl
from jax.experimental.pallas import tpu as pltpu
from jax.sharding import PartitionSpec as P

MESH = pl.DeviceIdType.MESH
F32 = jnp.float32
BF16 = jnp.bfloat16
NX, NY, NZ = 4, 4, 4


def split(value):
    hi = value.astype(BF16)
    lo = (value - hi.astype(F32)).astype(BF16)
    return hi, lo


def kernel(rows, own, offs, out, corr, g, of, tsel, sl, tl, sb, tb, ls, lt, rs, rt, pacc, qacc, part, parts,
           ssem, rsem, psem, trsem, lsem):
    half = 4 * rows
    tm = lax.axis_index("tm")
    mode = lax.axis_index("mode")
    a = tm % 2
    x = (tm // 2) % NX
    zl = tm // (2 * NX)
    y = mode % NY
    h = mode // NY

    def dev(core=a, xx=x, zz=zl, yy=y, hh=h):
        return ((zz * NX + xx) * 2 + core, hh * NY + yy)

    def step(v, d, n=4):
        return (v + d + n) % n

    sib = dev(core=1 - a)

    bar = pltpu.get_barrier_semaphore()
    count = 0
    for dc in range(2):
        for dh in range(2):
            for dy in range(4):
                if dc or dh or dy:
                    pl.semaphore_signal(bar, 1, device_id=dev(core=(a + dc) % 2, yy=step(y, dy), hh=(h + dh) % 2), device_id_type=MESH)
                    count += 1
    for d in (1, 2, 3):
        pl.semaphore_signal(bar, 1, device_id=dev(xx=step(x, d)), device_id_type=MESH)
        count += 1
    for d in (1, 3):
        pl.semaphore_signal(bar, 1, device_id=dev(zz=step(zl, d)), device_id_type=MESH)
        count += 1
    for k in range(2):
        of[a, k] = jnp.full(of.shape[2:], offs[0, k].astype(F32), F32)
    pl.semaphore_wait(bar, count)

    sends = []
    counter = [0]

    def remote(src, dst, device, start=True, when=None, rsem_at=None):
        i = counter[0]
        counter[0] += 1
        cp = pltpu.make_async_remote_copy(
            src_ref=src, dst_ref=dst, send_sem=ssem.at[i], recv_sem=rsem.at[i] if rsem_at is None else rsem_at,
            device_id=device, device_id_type=MESH)
        if when is None:
            cp.start()
        else:
            pl.when(when)(cp.start)
        sends.append((cp, when))
        return cp

    def local(src, dst, i):
        cp = pltpu.make_async_copy(src, dst, lsem.at[i])
        cp.start()
        return cp

    mine = pl.ds(pl.multiple_of(a * half, half), half)
    other = pl.ds(pl.multiple_of((1 - a) * half, half), half)

    sib_of = remote(of.at[a], of.at[a], sib)
    sib_g = remote(own.at[:, :, other], g.at[0, a], sib)
    keep = local(own.at[:, :, mine], g.at[0, a], 0)
    keep.wait()
    sib_g.wait_recv()

    wrap = x < 2
    d1, d2 = dev(xx=step(x, -1)), dev(xx=step(x, -2))
    wrap1 = x < 1
    nowrap1, nowrap2 = x >= 1, x >= 2
    up = dev(zz=step(zl, -1))

    def shift_z(u):
        return remote(g.at[u, 0:2], g.at[u, 6:8], up, when=wrap)

    def shift_x(u, field_at, first, second):
        r1, r2 = first
        w1, w2 = second
        return (remote(g.at[u, field_at:field_at + 2], g.at[u, 2:4], d1, when=w1, rsem_at=r1),
                remote(g.at[u, field_at:field_at + 2], g.at[u, 4:6], d2, when=w2, rsem_at=r2))

    def spread_s(u):
        cps = []
        for d in (1, 2, 3):
            yd = step(y, d)
            dst = sl.at[a, y] if u == 0 else sb.at[y]
            cps.append(remote(g.at[u, yd // 2], dst, dev(yy=yd)))
        return cps

    def spread_t(u):
        cps = []
        for d in (1, 2, 3):
            yd = step(y, d)
            dst = tl.at[a, y] if u == 0 else tb.at[y]
            cps.append(remote(tsel.at[u, yd], dst, dev(yy=yd)))
        return cps

    xsem = [(psem.at[4 + 2 * u], psem.at[5 + 2 * u]) for u in range(2)]
    z0 = shift_z(0)
    x0 = shift_x(0, 0, xsem[0], (nowrap1, nowrap2))
    s0 = spread_s(0)
    own_s0 = local(g.at[0, y // 2], sl.at[a, y], 1)
    cross = remote(g.at[0, 0:2], g.at[1, 0:2], dev(hh=1 - h))
    pl.when(wrap)(z0.wait_recv)
    w0 = shift_x(0, 6, xsem[0], (wrap1, wrap))
    sib_of.wait_recv()

    def forward(dst, index):
        return remote(dst.at[a, index], dst.at[a, index], sib)

    own_s0.wait()
    fs = [forward(sl, y)]
    for d in (1, 2, 3):
        s0[d - 1].wait_recv()
        fs.append(forward(sl, step(y, -d)))

    def select(u):
        def body(i, carry):
            ri = i // (rows // 8)
            at = pl.ds(pl.multiple_of((i % (rows // 8)) * 8, 8), 8)
            cand = [g[u, f, ri, at, :] for f in range(1, 6)]
            for p in range(4):
                first = p // 2
                m = of[first, p % 2]
                v = cand[first + 3]
                for o in (3, 2, 1):
                    v = jnp.where(m == F32(o), cand[first + o - 1], v)
                tsel[u, p, ri, at, :] = v
            return carry
        lax.fori_loop(0, 2 * rows // 8, body, 0)

    x0[0].wait_recv()
    x0[1].wait_recv()
    select(0)
    t0 = spread_t(0)
    own_t0 = local(tsel.at[0, y], tl.at[a, y], 2)

    cross.wait_recv()
    z1 = shift_z(1)
    x1 = shift_x(1, 0, xsem[1], (nowrap1, nowrap2))
    s1 = spread_s(1)
    own_s1 = local(g.at[1, y // 2], sb.at[y], 3)
    pl.when(wrap)(z1.wait_recv)
    w1 = shift_x(1, 6, xsem[1], (wrap1, wrap))

    own_t0.wait()
    ft = [forward(tl, y)]
    for d in (1, 2, 3):
        t0[d - 1].wait_recv()
        ft.append(forward(tl, step(y, -d)))

    def prepare_left(src, dst, ch, yi):
        at = pl.ds(pl.multiple_of(yi * rows, rows), rows)
        for ri in range(2):
            for yb in range(4):
                hi, lo = split(src[ch, yi, ri, :, yb * rows:(yb + 1) * rows])
                cols = slice((2 * yb + ri) * rows, (2 * yb + ri + 1) * rows)
                dst[0, ch, at, cols] = hi
                dst[1, ch, at, cols] = lo

    def prepare_right(block, dst, yi):
        at0 = pl.ds(pl.multiple_of(yi * 2 * rows, rows), rows)
        at1 = pl.ds(pl.multiple_of(yi * 2 * rows + rows, rows), rows)
        rh, rl = split(block[0])
        ih, il = split(block[1])
        for part_at, re, im in ((0, rh, ih), (1, rl, il)):
            dst[part_at, 0, at0, :] = re
            dst[part_at, 0, at1, :] = -im
            dst[part_at, 1, at0, :] = im
            dst[part_at, 1, at1, :] = re

    tile_m, tile_n = 2 * rows, 2 * rows

    def multiply(left, ch, right, acc, fresh):
        def body(i, carry):
            ri = i // 4
            mt = pl.ds(pl.multiple_of(((i // 2) % 2) * tile_m, tile_m), tile_m)
            nt = pl.ds(pl.multiple_of((i % 2) * tile_n, tile_n), tile_n)
            lh = left[0, ch, mt, :]
            ll = left[1, ch, mt, :]
            rh = right[0, ri, :, nt]
            rl = right[1, ri, :, nt]
            r = jnp.dot(lh, rh, preferred_element_type=F32)
            r += jnp.dot(lh, rl, preferred_element_type=F32)
            r += jnp.dot(ll, rh, preferred_element_type=F32)
            if fresh:
                acc[ri, mt, nt] = r
            else:
                acc[ri, mt, nt] += r
            return carry
        lax.fori_loop(0, 8, body, 0)

    def each_block(fn):
        def body(i, carry):
            fn(i)
            return carry
        lax.fori_loop(0, 4, body, 0)

    for cp in fs:
        cp.wait_recv()

    def prep_s(i):
        prepare_left(sl, ls, 0, i)
        prepare_left(sl, ls, 1, i)
        prepare_right(sl.at[a, i], rs, i)
    each_block(prep_s)

    for cp in ft:
        cp.wait_recv()

    def prep_t(i):
        prepare_left(tl, lt, 0, i)
        prepare_left(tl, lt, 1, i)
        prepare_right(tl.at[a, i], rt, i)
    each_block(prep_t)

    multiply(ls, h, rt, pacc, True)
    multiply(lt, h, rs, qacc, True)

    x1[0].wait_recv()
    x1[1].wait_recv()
    select(1)
    t1 = spread_t(1)
    own_t1 = local(tsel.at[1, y], tb.at[y], 4)

    own_s1.wait()
    for cp in s1:
        cp.wait_recv()
    each_block(lambda i: prepare_right(sb.at[i], rs, i))
    multiply(lt, 1 - h, rs, qacc, False)

    own_t1.wait()
    for cp in t1:
        cp.wait_recv()
    each_block(lambda i: prepare_right(tb.at[i], rt, i))
    multiply(ls, 1 - h, rt, pacc, False)

    src_core = y // 2
    k = y % 2
    home = src_core == a
    away = src_core != a
    for d in range(4):
        yd = step(y, d)
        src = pacc.at[:, pl.ds(pl.multiple_of(yd * rows, rows), rows), :]
        dst = out.at[k, :, :, mine]
        if d == 0:
            lcp = pltpu.make_async_copy(src, dst, lsem.at[5])
            pl.when(home)(lcp.start)
            remote(src, dst, sib, when=away, rsem_at=psem.at[2 * k + a])
        else:
            remote(src, dst, dev(core=src_core, yy=yd), rsem_at=psem.at[2 * k + a])

    def tr_body(i, acc):
        ri = i // (4 * rows // 8)
        at = pl.ds(pl.multiple_of((i % (4 * rows // 8)) * 8, 8), 8)
        return acc + pacc[ri, at, :] * qacc[ri, at, :]
    acc = lax.fori_loop(0, 2 * 4 * rows // 8, tr_body, jnp.zeros((8, half), F32))
    lanes = part.shape[1]
    tot = acc[:, 0:lanes]
    for j in range(1, half // lanes):
        tot += acc[:, j * lanes:(j + 1) * lanes]
    part[...] = tot
    slot = 2 * h + a
    for dh in range(2):
        for d in range(4):
            dst = parts.at[k, slot]
            if d == 0 and dh == 0:
                @pl.when(home)
                def _():
                    parts[k, slot] = part[...]
                remote(part, dst, sib, when=away, rsem_at=trsem.at[k, slot])
            else:
                remote(part, dst, dev(core=src_core, yy=step(y, d), hh=(h + dh) % 2), rsem_at=trsem.at[k, slot])

    for kk in range(2):
        for ch in range(2):
            for hh in range(2):
                i = 2 * hh + ch
                own_slot = (y == 2 * a + kk) & (ch == a) & (hh == h)
                cp = pltpu.make_async_remote_copy(src_ref=part, dst_ref=parts.at[kk, i], send_sem=ssem.at[0], recv_sem=trsem.at[kk, i], device_id=sib, device_id_type=MESH)
                pl.when(jnp.logical_not(own_slot))(cp.wait_recv)
    width = F32(8 * rows)
    for kk in range(2):
        total = parts[kk, 0] + parts[kk, 1] + parts[kk, 2] + parts[kk, 3]
        corr[kk] = jnp.broadcast_to(jnp.sum(total) / width, corr.shape[1:])

    for kk in range(2):
        for ch in range(2):
            own_slot = (y == 2 * a + kk) & (ch == a)
            cp = pltpu.make_async_remote_copy(
                src_ref=pacc.at[:, 0:rows, :], dst_ref=out.at[kk, :, :, ch * half:(ch + 1) * half],
                send_sem=ssem.at[0], recv_sem=psem.at[2 * kk + ch], device_id=sib, device_id_type=MESH)
            pl.when(jnp.logical_not(own_slot))(cp.wait_recv)
    pl.when(home)(lcp.wait)
    for cp, when in sends:
        if when is None:
            cp.wait_send()
        else:
            pl.when(when)(cp.wait_send)


NSEM = 64


def body(fields, offsets):
    own = fields[0]
    rows, width = own.shape[1], own.shape[2]
    half = width // 2
    block = (2, rows, half)
    out, corr = pl.pallas_call(
        functools.partial(kernel, rows),
        out_shape=(jax.ShapeDtypeStruct((2, 2, rows, width), F32), jax.ShapeDtypeStruct((2, 8, 128), F32)),
        in_specs=[pl.BlockSpec(memory_space=pl.ANY), pl.BlockSpec(memory_space=pltpu.SMEM)],
        out_specs=(pl.BlockSpec(memory_space=pl.ANY), pl.BlockSpec(memory_space=pltpu.VMEM)),
        scratch_shapes=[
            pltpu.VMEM((2, 8) + block, F32),
            pltpu.VMEM((2, 2, 8, half), F32),
            pltpu.VMEM((2, 4) + block, F32),
            pltpu.VMEM((2, 4) + block, F32),
            pltpu.VMEM((2, 4) + block, F32),
            pltpu.VMEM((4,) + block, F32),
            pltpu.VMEM((4,) + block, F32),
            pltpu.VMEM((2, 2, half, width), BF16),
            pltpu.VMEM((2, 2, half, width), BF16),
            pltpu.VMEM((2, 2, width, half), BF16),
            pltpu.VMEM((2, 2, width, half), BF16),
            pltpu.VMEM((2, half, half), F32),
            pltpu.VMEM((2, half, half), F32),
            pltpu.VMEM((8, 128), F32),
            pltpu.VMEM((2, 4, 8, 128), F32),
            pltpu.SemaphoreType.DMA((NSEM,)),
            pltpu.SemaphoreType.DMA((NSEM,)),
            pltpu.SemaphoreType.DMA((8,)),
            pltpu.SemaphoreType.DMA((2, 4)),
            pltpu.SemaphoreType.DMA((8,)),
        ],
        compiler_params=pltpu.CompilerParams(collective_id=0, has_side_effects=True, vmem_limit_bytes=60 * 2**20),
        cost_estimate=pl.CostEstimate(flops=13 * 10**9, bytes_accessed=4 * 2**20, transcendentals=0),
        name="contract",
    )(own, offsets)
    return out[None], corr[:, 0, 0][None]


def solution(mesh):
    in_specs = (P("tm", None, "mode", None), P("tm", None))
    out_specs = (P("tm", None, None, "mode", None), P("tm", None))
    return jax.shard_map(body, mesh=mesh, in_specs=in_specs, out_specs=out_specs, check_vma=False)
```

```python
import functools

import jax
import jax.numpy as jnp
from jax import lax
from jax.experimental import pallas as pl
from jax.experimental.pallas import tpu as pltpu
from jax.sharding import PartitionSpec as P

MESH = pl.DeviceIdType.MESH
F32 = jnp.float32
BF16 = jnp.bfloat16
NX, NY, NC = 4, 4, 4
NSEM = 192


def split(value):
    hi = value.astype(BF16)
    lo = (value - hi.astype(F32)).astype(BF16)
    return hi, lo


def kernel(rows, own, offs, out, corr, g, of, tsel, sl, tl, sb, tb, ls, lt, rs, rt, pacc, qacc, part, parts,
           ssem, rsem, xsem, psem, trsem, lsem):
    wide = 128
    half = NC * wide
    tm = lax.axis_index("tm")
    mode = lax.axis_index("mode")
    a = tm % 2
    x = (tm // 2) % NX
    zl = tm // (2 * NX)
    y = mode % NY
    h = mode // NY

    def dev(core=a, xx=x, zz=zl, yy=y, hh=h):
        return ((zz * NX + xx) * 2 + core, hh * NY + yy)

    def step(v, d):
        return (v + d + 4) % 4

    sib = dev(core=1 - a)

    bar = pltpu.get_barrier_semaphore()
    count = 0

    def greet(device):
        pl.semaphore_signal(bar, 1, device_id=device, device_id_type=MESH)

    for dh in (1, 0):
        for dc in range(2):
            for dy in range(4):
                if dc or dh or dy:
                    greet(dev(core=(a + dc) % 2, yy=step(y, dy), hh=(h + dh) % 2))
                    count += 1
    for d in (1, 3):
        greet(dev(zz=step(zl, d)))
        count += 1
    for d in (1, 2, 3):
        greet(dev(xx=step(x, d)))
        count += 1

    def columns(core, c):
        return pl.ds(pl.multiple_of(core * half + c * wide, wide), wide)

    nlocal = [0]

    def local(src, dst):
        cp = pltpu.make_async_copy(src, dst, lsem.at[nlocal[0]])
        nlocal[0] += 1
        cp.start()
        return cp

    keep = [local(own.at[:, :, columns(a, c)], g.at[0, c, a]) for c in range(NC)]
    for k in range(2):
        of[a, k] = jnp.full(of.shape[2:], offs[0, k].astype(F32), F32)
    pl.semaphore_wait(bar, count)

    sends = []
    counter = [0]

    def remote(src, dst, device, when=None, at=None):
        i = counter[0]
        counter[0] += 1
        cp = pltpu.make_async_remote_copy(
            src_ref=src, dst_ref=dst, send_sem=ssem.at[i], recv_sem=rsem.at[i] if at is None else at,
            device_id=device, device_id_type=MESH)
        if when is None:
            cp.start()
        else:
            pl.when(when)(cp.start)
        sends.append((cp, when))
        return cp

    sib_of = remote(of.at[a], of.at[a], sib)
    sib_g = [remote(own.at[:, :, columns(1 - a, c)], g.at[0, c, a], sib) for c in range(NC)]

    wrap1, wrap2 = x < 1, x < 2
    plain1, plain2 = x >= 1, x >= 2
    d1, d2, up, across = dev(xx=step(x, -1)), dev(xx=step(x, -2)), dev(zz=step(zl, -1)), dev(hh=1 - h)

    def shift_z(u, c):
        return remote(g.at[u, c, 0:2], g.at[u, c, 6:8], up, when=wrap2)

    def shift_x(u, c, field, when1, when2):
        cp1 = remote(g.at[u, c, field:field + 2], g.at[u, c, 2:4], d1, when=when1, at=xsem.at[u, c, 0])
        cp2 = remote(g.at[u, c, field:field + 2], g.at[u, c, 4:6], d2, when=when2, at=xsem.at[u, c, 1])
        return cp1, cp2

    def spread(src, dst):
        return [remote(src(step(y, d)), dst, dev(yy=step(y, d))) for d in (1, 2, 3)]

    def wait_all(cps):
        for cp in cps:
            cp.wait_recv()

    def select(u, c):
        def body(i, carry):
            at = pl.ds(pl.multiple_of(i * 8, 8), 8)
            for ri in range(2):
                cand = [g[u, c, f, ri, at, :] for f in range(1, 6)]
                for p in range(4):
                    first = p // 2
                    m = of[first, p % 2]
                    v = cand[first + 3]
                    for o in (3, 2, 1):
                        v = jnp.where(m == F32(o), cand[first + o - 1], v)
                    tsel[u, c, p, ri, at, :] = v
            return carry
        lax.fori_loop(0, rows // 8, body, 0)

    z, xc, s0, t0, cross, s1, t1 = {}, {}, [], {}, {}, {}, {}
    for c in range(NC):
        keep[c].wait()
        sib_g[c].wait_recv()
        z[0, c] = shift_z(0, c)
        xc[0, c] = shift_x(0, c, 0, plain1, plain2)
        cross[c] = remote(g.at[0, c, 0:2], g.at[1, c, 0:2], across)
    s0 = spread(lambda yd: g.at[0, :, yd // 2], sl.at[a, y])
    own_s0 = local(g.at[0, :, y // 2], sl.at[a, y])
    sib_of.wait_recv()
    own_t0, own_s1, own_t1 = [], [], []
    fs, ft = [], []
    for c in range(NC):
        pl.when(wrap2)(z[0, c].wait_recv)
        shift_x(0, c, 6, wrap1, wrap2)
        wait_all(xc[0, c])
        select(0, c)
        t0[c] = spread(lambda yd: tsel.at[0, c, yd], tl.at[a, y, c])
        own_t0.append(local(tsel.at[0, c, y], tl.at[a, y, c]))
        cross[c].wait_recv()
        z[1, c] = shift_z(1, c)
        xc[1, c] = shift_x(1, c, 0, plain1, plain2)
        s1[c] = spread(lambda yd: g.at[1, c, yd // 2], sb.at[y, c])
        own_s1.append(local(g.at[1, c, y // 2], sb.at[y, c]))

    def forward(dst, index):
        return remote(dst.at[a, index], dst.at[a, index], sib)

    own_s0.wait()
    fs.append(forward(sl, y))
    for d in (1, 2, 3):
        s0[d - 1].wait_recv()
        fs.append(forward(sl, step(y, -d)))

    def prepare_left(src, dst, ch, yi):
        at = pl.ds(pl.multiple_of(yi * rows, rows), rows)
        for ri in range(2):
            for c in range(NC):
                hi, lo = split(src[ch, yi, c, ri])
                cols = slice((2 * c + ri) * wide, (2 * c + ri + 1) * wide)
                dst[0, ch, at, cols] = hi
                dst[1, ch, at, cols] = lo

    def prepare_right(src, dst, yi, c):
        at0 = pl.ds(pl.multiple_of(yi * 2 * rows, rows), rows)
        at1 = pl.ds(pl.multiple_of(yi * 2 * rows + rows, rows), rows)
        rh, rl = split(src[yi, c, 0])
        ih, il = split(src[yi, c, 1])
        for n, re, im in ((0, rh, ih), (1, rl, il)):
            dst[n, c, at0, 0:wide] = re
            dst[n, c, at0, wide:2 * wide] = im
            dst[n, c, at1, 0:wide] = -im
            dst[n, c, at1, wide:2 * wide] = re

    tile = 2 * rows

    def multiply(left, ch, right, acc, fresh, first, last):
        def body(i, carry):
            c = i // 2
            mt = pl.ds(pl.multiple_of((i % 2) * tile, tile), tile)
            lh = left[0, ch, mt, :]
            rh = right[0, c]
            r = jnp.dot(lh, rh, preferred_element_type=F32)
            r += jnp.dot(lh, right[1, c], preferred_element_type=F32)
            r += jnp.dot(left[1, ch, mt, :], rh, preferred_element_type=F32)
            for ri in range(2):
                v = r[:, ri * wide:(ri + 1) * wide]
                acc[c, ri, mt, :] = v if fresh else acc[c, ri, mt, :] + v
            return carry
        lax.fori_loop(2 * first, 2 * last, body, 0)

    def loop(n, fn):
        def body(i, carry):
            fn(i)
            return carry
        lax.fori_loop(0, n, body, 0)

    def prep_s(i):
        prepare_left(sl, ls, 0, i)
        prepare_left(sl, ls, 1, i)

    def prep_t(i):
        prepare_left(tl, lt, 0, i)
        prepare_left(tl, lt, 1, i)

    for c in range(NC):
        pl.when(wrap2)(z[1, c].wait_recv)
        shift_x(1, c, 6, wrap1, wrap2)
        wait_all(xc[1, c])
        select(1, c)
        t1[c] = spread(lambda yd: tsel.at[1, c, yd], tb.at[y, c])
        own_t1.append(local(tsel.at[1, c, y], tb.at[y, c]))
        if c == 0:
            for cp in own_t0:
                cp.wait()
            ft.append(forward(tl, y))
            for d in (1, 2, 3):
                for cc in range(NC):
                    t0[cc][d - 1].wait_recv()
                ft.append(forward(tl, step(y, -d)))
            wait_all(fs)
            loop(4, prep_s)
            loop(16, lambda i: prepare_right(sl.at[a], rs, i // NC, i % NC))
        if c == 1:
            wait_all(ft)
            loop(4, prep_t)
            loop(16, lambda i: prepare_right(tl.at[a], rt, i // NC, i % NC))
            multiply(ls, h, rt, pacc, True, 0, NC)
        if c == 2:
            multiply(lt, h, rs, qacc, True, 0, NC)

    for c in range(NC):
        own_s1[c].wait()
        wait_all(s1[c])
    loop(16, lambda i: prepare_right(sb, rs, i // NC, i % NC))
    multiply(lt, 1 - h, rs, qacc, False, 0, NC)

    src_core = y // 2
    k = y % 2
    home = src_core == a
    away = src_core != a
    total = jnp.zeros((8, wide), F32)
    back = []
    for c in range(NC):
        own_t1[c].wait()
        wait_all(t1[c])
        loop(4, lambda i: prepare_right(tb, rt, i, c))
        multiply(ls, 1 - h, rt, pacc, False, c, c + 1)
        for d in (1, 2, 3, 0):
            yd = step(y, d)
            src = pacc.at[c, :, pl.ds(pl.multiple_of(yd * rows, rows), rows), :]
            dst = out.at[k, :, :, columns(a, c)]
            if d == 0:
                lcp = pltpu.make_async_copy(src, dst, lsem.at[20 + c])
                pl.when(home)(lcp.start)
                back.append(lcp)
                remote(src, dst, sib, when=away, at=psem.at[k, a, c])
            else:
                remote(src, dst, dev(core=src_core, yy=yd), at=psem.at[k, a, c])

        def tr_body(i, acc):
            at = pl.ds(pl.multiple_of(i * 8, 8), 8)
            for ri in range(2):
                acc = acc + pacc[c, ri, at, :] * qacc[c, ri, at, :]
            return acc
        total = lax.fori_loop(0, 4 * rows // 8, tr_body, total)

    part[...] = total
    slot = 2 * h + a
    for dh in (1, 0):
        for d in (1, 2, 3, 0):
            dst = parts.at[k, slot]
            if d == 0 and dh == 0:
                @pl.when(home)
                def _():
                    parts[k, slot] = part[...]
                remote(part, dst, sib, when=away, at=trsem.at[k, slot])
            else:
                remote(part, dst, dev(core=src_core, yy=step(y, d), hh=(h + dh) % 2), at=trsem.at[k, slot])

    def expect(dst, sem, unless):
        cp = pltpu.make_async_remote_copy(src_ref=dst, dst_ref=dst, send_sem=ssem.at[0], recv_sem=sem, device_id=sib, device_id_type=MESH)
        pl.when(jnp.logical_not(unless))(cp.wait_recv)

    for kk in range(2):
        for ch in range(2):
            for hh in range(2):
                expect(parts.at[kk, 2 * hh + ch], trsem.at[kk, 2 * hh + ch], (y == 2 * a + kk) & (ch == a) & (hh == h))
    width = F32(8 * rows)
    for kk in range(2):
        trace = parts[kk, 0] + parts[kk, 1] + parts[kk, 2] + parts[kk, 3]
        corr[kk] = jnp.broadcast_to(jnp.sum(trace) / width, corr.shape[1:])

    for kk in range(2):
        for ch in range(2):
            for c in range(NC):
                expect(out.at[kk, :, :, columns(ch, c)], psem.at[kk, ch, c], (y == 2 * a + kk) & (ch == a))
    for lcp in back:
        pl.when(home)(lcp.wait)
    for cp, when in sends:
        if when is None:
            cp.wait_send()
        else:
            pl.when(when)(cp.wait_send)


def body(fields, offsets):
    own = fields[0]
    rows, width = own.shape[1], own.shape[2]
    half = width // 2
    block = (2, rows, 128)
    out, corr = pl.pallas_call(
        functools.partial(kernel, rows),
        out_shape=(jax.ShapeDtypeStruct((2, 2, rows, width), F32), jax.ShapeDtypeStruct((2, 8, 128), F32)),
        in_specs=[pl.BlockSpec(memory_space=pl.ANY), pl.BlockSpec(memory_space=pltpu.SMEM)],
        out_specs=(pl.BlockSpec(memory_space=pl.ANY), pl.BlockSpec(memory_space=pltpu.VMEM)),
        scratch_shapes=[
            pltpu.VMEM((2, NC, 8) + block, F32),
            pltpu.VMEM((2, 2, 8, 128), F32),
            pltpu.VMEM((2, NC, 4) + block, F32),
            pltpu.VMEM((2, 4, NC) + block, F32),
            pltpu.VMEM((2, 4, NC) + block, F32),
            pltpu.VMEM((4, NC) + block, F32),
            pltpu.VMEM((4, NC) + block, F32),
            pltpu.VMEM((2, 2, half, width), BF16),
            pltpu.VMEM((2, 2, half, width), BF16),
            pltpu.VMEM((2, NC, width, 256), BF16),
            pltpu.VMEM((2, NC, width, 256), BF16),
            pltpu.VMEM((NC, 2, half, 128), F32),
            pltpu.VMEM((NC, 2, half, 128), F32),
            pltpu.VMEM((8, 128), F32),
            pltpu.VMEM((2, 4, 8, 128), F32),
            pltpu.SemaphoreType.DMA((NSEM,)),
            pltpu.SemaphoreType.DMA((NSEM,)),
            pltpu.SemaphoreType.DMA((2, NC, 2)),
            pltpu.SemaphoreType.DMA((2, 2, NC)),
            pltpu.SemaphoreType.DMA((2, 4)),
            pltpu.SemaphoreType.DMA((24,)),
        ],
        compiler_params=pltpu.CompilerParams(collective_id=0, has_side_effects=True, vmem_limit_bytes=60 * 2**20),
        cost_estimate=pl.CostEstimate(flops=13 * 10**9, bytes_accessed=4 * 2**20, transcendentals=0),
        name="contract",
    )(own, offsets)
    return out[None], corr[:, 0, 0][None]


def solution(mesh):
    in_specs = (P("tm", None, "mode", None), P("tm", None))
    out_specs = (P("tm", None, None, "mode", None), P("tm", None))
    return jax.shard_map(body, mesh=mesh, in_specs=in_specs, out_specs=out_specs, check_vma=False)
```

```python
import functools

import jax
import jax.numpy as jnp
from jax import lax
from jax.experimental import pallas as pl
from jax.experimental.pallas import tpu as pltpu
from jax.sharding import PartitionSpec as P

MESH = pl.DeviceIdType.MESH
F32 = jnp.float32
BF16 = jnp.bfloat16
NX, NY, NC = 4, 4, 4
NSEM = 224
VIA_HIGH, VIA_LOW = (0, 1), (2, 3)


def split(value):
    hi = value.astype(BF16)
    lo = (value - hi.astype(F32)).astype(BF16)
    return hi, lo


def kernel(rows, own, offs, out, corr, g, of, tsel, sl, tl, sb, tb, ls, lt, rs, rt, pacc, qacc, part, parts,
           ssem, rsem, bsem, xsem, psem, trsem, lsem):
    wide = 128
    half = NC * wide
    tm = lax.axis_index("tm")
    mode = lax.axis_index("mode")
    a = tm % 2
    x = (tm // 2) % NX
    zl = tm // (2 * NX)
    y = mode % NY
    h = mode // NY

    def dev(core=a, xx=x, zz=zl, yy=y, hh=h):
        return ((zz * NX + xx) * 2 + core, hh * NY + yy)

    def step(v, d):
        return (v + d + 4) % 4

    sib = dev(core=1 - a)

    bar = pltpu.get_barrier_semaphore()
    count = 0

    def greet(device):
        pl.semaphore_signal(bar, 1, device_id=device, device_id_type=MESH)

    for dh in (1, 0):
        for dc in range(2):
            for dy in range(4):
                if dc or dh or dy:
                    greet(dev(core=(a + dc) % 2, yy=step(y, dy), hh=(h + dh) % 2))
                    count += 1
    for dz in (1, -1):
        greet(dev(zz=step(zl, dz)))
        greet(dev(xx=step(x, -dz), zz=step(zl, dz)))
        count += 2
    for d in (1, 2, 3):
        greet(dev(xx=step(x, d)))
        count += 1

    def columns(core, c):
        return pl.ds(pl.multiple_of(core * half + c * wide, wide), wide)

    nlocal = [0]

    def begin(cp, when):
        if when is None:
            cp.start()
        else:
            pl.when(when)(cp.start)

    def local(src, dst, when=None, at=None):
        if at is None:
            at = nlocal[0]
            nlocal[0] += 1
        cp = pltpu.make_async_copy(src, dst, lsem.at[at])
        begin(cp, when)
        return cp

    keep = [local(own.at[:, :, columns(a, c)], g.at[0, c, a]) for c in range(NC)]
    for k in range(2):
        of[a, k] = jnp.full(of.shape[2:], offs[0, k].astype(F32), F32)
    pl.semaphore_wait(bar, count)

    sends = []
    counter = [0]

    def remote(src, dst, device, when=None, at=None):
        i = counter[0]
        counter[0] += 1
        cp = pltpu.make_async_remote_copy(
            src_ref=src, dst_ref=dst, send_sem=ssem.at[i], recv_sem=rsem.at[i] if at is None else at,
            device_id=device, device_id_type=MESH)
        begin(cp, when)
        sends.append((cp, when))
        return cp

    sib_of = remote(of.at[a], of.at[a], sib)
    sib_g = [remote(own.at[:, :, columns(1 - a, c)], g.at[0, c, a], sib) for c in range(NC)]

    low, high, second, last = x < 2, x >= 2, x == 2, x == 3
    d1, d2, up, across = dev(xx=step(x, -1)), dev(xx=step(x, -2)), dev(zz=step(zl, -1)), dev(hh=1 - h)
    firsts, seconds, behind, lent = {}, {}, {}, {}

    def to_first(u, c, field, when):
        firsts[u, c] = remote(g.at[u, c, field:field + 2], g.at[u, c, 2:4], d1, when=when, at=xsem.at[u, c, 0])

    def to_second(u, c, field, when):
        seconds[u, c] = remote(g.at[u, c, field:field + 2], g.at[u, c, 4:6], d2, when=when, at=xsem.at[u, c, 1])

    def relay_first(u, c, when):
        remote(g.at[u, c, 2:4], g.at[u, c, 4:6], dev(xx=step(x, -1)), when=when, at=xsem.at[u, c, 1])

    def shift_z(u, c, when):
        behind[u, c] = remote(g.at[u, c, 0:2], g.at[u, c, 6:8], up, when=when)

    def lend(u, c, when):
        lent[u, c] = remote(g.at[u, c, 0:2], g.at[u, c, 6:8], dev(xx=3 - x), when=when)

    def pass_back(u, c):
        pl.when(high)(lent[u, c].wait_recv)
        at = jnp.where(last, 0, 1)
        remote(g.at[u, c, 6:8], g.at[u, c, pl.ds(2 + 2 * at, 2)], dev(xx=3, zz=step(zl, -1)), when=high, at=xsem.at[u, c, at])

    def hand_on(u, c, when):
        pl.when(when)(firsts[u, c].wait_recv)
        relay_first(u, c, when)

    def bring_on(u, c):
        pl.when(low)(behind[u, c].wait_recv)
        to_first(u, c, 6, x == 0)
        to_second(u, c, 6, low)

    def arrived_first(u, c):
        if c in VIA_LOW:
            if u == 0:
                bring_on(u, c)
            firsts[u, c].wait_recv()
        else:
            pl.when(low)(firsts[u, c].wait_recv)

    def spread(src, dst, when=None, at=None):
        return [remote(src(step(y, d)), dst, dev(yy=step(y, d)), when=when, at=None if at is None else at(d)) for d in (1, 2, 3)]

    def wait_all(cps):
        for cp in cps:
            cp.wait_recv()

    def select(u, c):
        def body(i, carry):
            at = pl.ds(pl.multiple_of(i * 8, 8), 8)
            for ri in range(2):
                cand = [g[u, c, f, ri, at, :] for f in range(1, 6)]
                for p in range(4):
                    first = p // 2
                    m = of[first, p % 2]
                    v = cand[first + 3]
                    for o in (3, 2, 1):
                        v = jnp.where(m == F32(o), cand[first + o - 1], v)
                    tsel[u, c, p, ri, at, :] = v
            return carry
        lax.fori_loop(0, rows // 8, body, 0)

    t0, cross, s1, t1 = {}, {}, {}, {}
    own_t0, own_s1, own_t1 = [], {}, []
    fs, ft = [], []

    def go_across(c):
        cross[c] = remote(g.at[0, c, 0:2], g.at[1, c, 0:2], across)

    for c in range(NC):
        keep[c].wait()
        sib_g[c].wait_recv()
        if c in VIA_HIGH:
            lend(0, c, low)
    for c in range(NC):
        to_first(0, c, 0, x >= 1)
        to_second(0, c, 0, second)
    s0 = spread(lambda yd: g.at[0, :, yd // 2], sl.at[a, y])
    own_s0 = local(g.at[0, :, y // 2], sl.at[a, y])
    for c in VIA_HIGH:
        pass_back(0, c)
        go_across(c)
    for c in VIA_LOW:
        shift_z(0, c, low)
        go_across(c)
    for c in VIA_HIGH:
        hand_on(0, c, high)
    for c in VIA_LOW:
        to_second(0, c, 0, last)
    sib_of.wait_recv()

    def crossed(c):
        cross[c].wait_recv()
        to_first(1, c, 0, x >= 1)
        to_second(1, c, 0, high if c in VIA_LOW else second)
        if c in VIA_LOW:
            shift_z(1, c, low)
        else:
            lend(1, c, low)
        s1[c] = spread(lambda yd: g.at[1, c, yd // 2], sb.at[y, c])
        own_s1[c] = local(g.at[1, c, y // 2], sb.at[y, c])

    for c in range(NC):
        arrived_first(0, c)
        seconds[0, c].wait_recv()
        select(0, c)
        t0[c] = spread(lambda yd: tsel.at[0, c, yd], tl.at[a, y, c])
        own_t0.append(local(tsel.at[0, c, y], tl.at[a, y, c]))
        crossed(c)
        if c >= 1:
            pass_back(1, c - 1) if c - 1 in VIA_HIGH else None
        if c >= 2:
            hand_on(1, c - 2, second)
    for c in VIA_HIGH:
        hand_on(1, c, last)

    def forward(dst, index):
        return remote(dst.at[a, index], dst.at[a, index], sib)

    own_s0.wait()
    fs.append(forward(sl, y))
    for d in (1, 2, 3):
        s0[d - 1].wait_recv()
        fs.append(forward(sl, step(y, -d)))

    def prepare_left(src, dst, ch, yi):
        at = pl.ds(pl.multiple_of(yi * rows, rows), rows)
        for ri in range(2):
            for c in range(NC):
                hi, lo = split(src[ch, yi, c, ri])
                cols = slice((2 * c + ri) * wide, (2 * c + ri + 1) * wide)
                dst[0, ch, at, cols] = hi
                dst[1, ch, at, cols] = lo

    def prepare_right(src, dst, yi, c):
        at0 = pl.ds(pl.multiple_of(yi * 2 * rows, rows), rows)
        at1 = pl.ds(pl.multiple_of(yi * 2 * rows + rows, rows), rows)
        rh, rl = split(src[yi, c, 0])
        ih, il = split(src[yi, c, 1])
        for n, re, im in ((0, rh, ih), (1, rl, il)):
            dst[n, c, at0, 0:wide] = re
            dst[n, c, at0, wide:2 * wide] = im
            dst[n, c, at1, 0:wide] = -im
            dst[n, c, at1, wide:2 * wide] = re

    def multiply(left, ch, right, acc, fresh, first, last):
        def body(c, carry):
            lh = left[0, ch]
            rh = right[0, c]
            r = jnp.dot(lh, rh, preferred_element_type=F32)
            r += jnp.dot(lh, right[1, c], preferred_element_type=F32)
            r += jnp.dot(left[1, ch], rh, preferred_element_type=F32)
            for ri in range(2):
                v = r[:, ri * wide:(ri + 1) * wide]
                acc[c, ri] = v if fresh else acc[c, ri] + v
            return carry
        lax.fori_loop(first, last, body, 0)

    def loop(n, fn):
        def body(i, carry):
            fn(i)
            return carry
        lax.fori_loop(0, n, body, 0)

    def prep_s(i):
        prepare_left(sl, ls, 0, i)
        prepare_left(sl, ls, 1, i)

    def prep_t(i):
        prepare_left(tl, lt, 0, i)
        prepare_left(tl, lt, 1, i)

    for cp in own_t0:
        cp.wait()
    ft.append(forward(tl, y))
    for d in (1, 2, 3):
        for cc in range(NC):
            t0[cc][d - 1].wait_recv()
        ft.append(forward(tl, step(y, -d)))

    def prep_left():
        loop(4, prep_s)
        loop(4, prep_t)
        loop(16, lambda i: prepare_right(sl.at[a], rs, i // NC, i % NC))
        loop(16, lambda i: prepare_right(tl.at[a], rt, i // NC, i % NC))

    wait_all(fs)
    wait_all(ft)

    for c in VIA_LOW:
        bring_on(1, c)

    @pl.when(high)
    def _():
        prep_left()
        multiply(ls, h, rt, pacc, True, 0, NC)
        multiply(lt, h, rs, qacc, True, 0, NC)

    for c in range(NC):
        arrived_first(1, c)
        seconds[1, c].wait_recv()
        select(1, c)
        t1[c] = spread(lambda yd: tsel.at[1, c, yd], tb.at[y, c])
        own_t1.append(local(tsel.at[1, c, y], tb.at[y, c]))
        if c == 1:
            pl.when(low)(prep_left)
        if c == 2:
            pl.when(low)(lambda: multiply(ls, h, rt, pacc, True, 0, NC))
        if c == 3:
            pl.when(low)(lambda: multiply(lt, h, rs, qacc, True, 0, NC))

    for c in range(NC):
        own_s1[c].wait()
        wait_all(s1[c])
    loop(16, lambda i: prepare_right(sb, rs, i // NC, i % NC))
    multiply(lt, 1 - h, rs, qacc, False, 0, NC)

    src_core = y // 2
    k = y % 2
    home = src_core == a
    away = src_core != a
    total = jnp.zeros((8, wide), F32)
    back = []
    for c in range(NC):
        own_t1[c].wait()
        wait_all(t1[c])
        loop(4, lambda i: prepare_right(tb, rt, i, c))
        multiply(ls, 1 - h, rt, pacc, False, c, c + 1)
        for d in (1, 2, 3, 0):
            yd = step(y, d)
            src = pacc.at[c, :, pl.ds(pl.multiple_of(yd * rows, rows), rows), :]
            dst = out.at[k, :, :, columns(a, c)]
            if d == 0:
                lcp = pltpu.make_async_copy(src, dst, lsem.at[20 + c])
                pl.when(home)(lcp.start)
                back.append(lcp)
                remote(src, dst, sib, when=away, at=psem.at[k, a, c])
            else:
                remote(src, dst, dev(core=src_core, yy=yd), at=psem.at[k, a, c])

        def tr_body(i, acc):
            at = pl.ds(pl.multiple_of(i * 8, 8), 8)
            for ri in range(2):
                acc = acc + pacc[c, ri, at, :] * qacc[c, ri, at, :]
            return acc
        total = lax.fori_loop(0, 4 * rows // 8, tr_body, total)

    part[...] = total
    slot = 2 * h + a
    for dh in (1, 0):
        for d in (1, 2, 3, 0):
            dst = parts.at[k, slot]
            if d == 0 and dh == 0:
                @pl.when(home)
                def _():
                    parts[k, slot] = part[...]
                remote(part, dst, sib, when=away, at=trsem.at[k, slot])
            else:
                remote(part, dst, dev(core=src_core, yy=step(y, d), hh=(h + dh) % 2), at=trsem.at[k, slot])

    def expect(dst, sem, unless):
        cp = pltpu.make_async_remote_copy(src_ref=dst, dst_ref=dst, send_sem=ssem.at[0], recv_sem=sem, device_id=sib, device_id_type=MESH)
        pl.when(jnp.logical_not(unless))(cp.wait_recv)

    for kk in range(2):
        for ch in range(2):
            for hh in range(2):
                expect(parts.at[kk, 2 * hh + ch], trsem.at[kk, 2 * hh + ch], (y == 2 * a + kk) & (ch == a) & (hh == h))
    width = F32(8 * rows)
    for kk in range(2):
        trace = parts[kk, 0] + parts[kk, 1] + parts[kk, 2] + parts[kk, 3]
        corr[kk] = jnp.broadcast_to(jnp.sum(trace) / width, corr.shape[1:])

    for kk in range(2):
        for ch in range(2):
            for c in range(NC):
                expect(out.at[kk, :, :, columns(ch, c)], psem.at[kk, ch, c], (y == 2 * a + kk) & (ch == a))
    for lcp in back:
        pl.when(home)(lcp.wait)
    for cp, when in sends:
        if when is None:
            cp.wait_send()
        else:
            pl.when(when)(cp.wait_send)


def body(fields, offsets):
    own = fields[0]
    rows, width = own.shape[1], own.shape[2]
    half = width // 2
    block = (2, rows, 128)
    out, corr = pl.pallas_call(
        functools.partial(kernel, rows),
        out_shape=(jax.ShapeDtypeStruct((2, 2, rows, width), F32), jax.ShapeDtypeStruct((2, 8, 128), F32)),
        in_specs=[pl.BlockSpec(memory_space=pl.ANY), pl.BlockSpec(memory_space=pltpu.SMEM)],
        out_specs=(pl.BlockSpec(memory_space=pl.ANY), pl.BlockSpec(memory_space=pltpu.VMEM)),
        scratch_shapes=[
            pltpu.VMEM((2, NC, 8) + block, F32),
            pltpu.VMEM((2, 2, 8, 128), F32),
            pltpu.VMEM((2, NC, 4) + block, F32),
            pltpu.VMEM((2, 4, NC) + block, F32),
            pltpu.VMEM((2, 4, NC) + block, F32),
            pltpu.VMEM((4, NC) + block, F32),
            pltpu.VMEM((4, NC) + block, F32),
            pltpu.VMEM((2, 2, half, width), BF16),
            pltpu.VMEM((2, 2, half, width), BF16),
            pltpu.VMEM((2, NC, width, 256), BF16),
            pltpu.VMEM((2, NC, width, 256), BF16),
            pltpu.VMEM((NC, 2, half, 128), F32),
            pltpu.VMEM((NC, 2, half, 128), F32),
            pltpu.VMEM((8, 128), F32),
            pltpu.VMEM((2, 4, 8, 128), F32),
            pltpu.SemaphoreType.DMA((NSEM,)),
            pltpu.SemaphoreType.DMA((NSEM,)),
            pltpu.SemaphoreType.DMA((NC, 3)),
            pltpu.SemaphoreType.DMA((2, NC, 2)),
            pltpu.SemaphoreType.DMA((2, 2, NC)),
            pltpu.SemaphoreType.DMA((2, 4)),
            pltpu.SemaphoreType.DMA((24,)),
        ],
        compiler_params=pltpu.CompilerParams(collective_id=0, has_side_effects=True, vmem_limit_bytes=60 * 2**20),
        cost_estimate=pl.CostEstimate(flops=13 * 10**9, bytes_accessed=4 * 2**20, transcendentals=0),
        name="contract",
    )(own, offsets)
    return out[None], corr[:, 0, 0][None]


def solution(mesh):
    in_specs = (P("tm", None, "mode", None), P("tm", None))
    out_specs = (P("tm", None, None, "mode", None), P("tm", None))
    return jax.shard_map(body, mesh=mesh, in_specs=in_specs, out_specs=out_specs, check_vma=False)
```

```python
import functools

import jax
import jax.numpy as jnp
from jax import lax
from jax.experimental import pallas as pl
from jax.experimental.pallas import tpu as pltpu
from jax.sharding import PartitionSpec as P

MESH = pl.DeviceIdType.MESH
F32 = jnp.float32
BF16 = jnp.bfloat16
NX, NY, NC = 4, 4, 4
NSEM = 224
VIA_HIGH, VIA_LOW = (0,), (1, 2, 3)


def split(value):
    hi = value.astype(BF16)
    lo = (value - hi.astype(F32)).astype(BF16)
    return hi, lo


def kernel(rows, own, offs, out, corr, g, of, tsel, sl, tl, sb, tb, ls, lt, rs, rt, pacc, qacc, part, parts,
           ssem, rsem, bsem, xsem, psem, trsem, lsem):
    wide = 128
    half = NC * wide
    tm = lax.axis_index("tm")
    mode = lax.axis_index("mode")
    a = tm % 2
    x = (tm // 2) % NX
    zl = tm // (2 * NX)
    y = mode % NY
    h = mode // NY

    def dev(core=a, xx=x, zz=zl, yy=y, hh=h):
        return ((zz * NX + xx) * 2 + core, hh * NY + yy)

    def step(v, d):
        return (v + d + 4) % 4

    sib = dev(core=1 - a)

    bar = pltpu.get_barrier_semaphore()
    count = 0

    def greet(device):
        pl.semaphore_signal(bar, 1, device_id=device, device_id_type=MESH)

    for dh in (1, 0):
        for dc in range(2):
            for dy in range(4):
                if dc or dh or dy:
                    greet(dev(core=(a + dc) % 2, yy=step(y, dy), hh=(h + dh) % 2))
                    count += 1
    for dz in (1, -1):
        greet(dev(zz=step(zl, dz)))
        greet(dev(xx=step(x, -dz), zz=step(zl, dz)))
        count += 2
    for d in (1, 2, 3):
        greet(dev(xx=step(x, d)))
        count += 1

    def columns(core, c):
        return pl.ds(pl.multiple_of(core * half + c * wide, wide), wide)

    nlocal = [0]

    def begin(cp, when):
        if when is None:
            cp.start()
        else:
            pl.when(when)(cp.start)

    def local(src, dst, when=None, at=None):
        if at is None:
            at = nlocal[0]
            nlocal[0] += 1
        cp = pltpu.make_async_copy(src, dst, lsem.at[at])
        begin(cp, when)
        return cp

    keep = [local(own.at[:, :, columns(a, c)], g.at[0, c, a]) for c in range(NC)]
    for k in range(2):
        of[a, k] = jnp.full(of.shape[2:], offs[0, k].astype(F32), F32)
    pl.semaphore_wait(bar, count)

    sends = []
    counter = [0]

    def remote(src, dst, device, when=None, at=None):
        i = counter[0]
        counter[0] += 1
        cp = pltpu.make_async_remote_copy(
            src_ref=src, dst_ref=dst, send_sem=ssem.at[i], recv_sem=rsem.at[i] if at is None else at,
            device_id=device, device_id_type=MESH)
        begin(cp, when)
        sends.append((cp, when))
        return cp

    sib_of = remote(of.at[a], of.at[a], sib)
    sib_g = [remote(own.at[:, :, columns(1 - a, c)], g.at[0, c, a], sib) for c in range(NC)]

    low, high, second, last = x < 2, x >= 2, x == 2, x == 3
    d1, d2, up, across = dev(xx=step(x, -1)), dev(xx=step(x, -2)), dev(zz=step(zl, -1)), dev(hh=1 - h)
    firsts, seconds, behind, lent = {}, {}, {}, {}

    def to_first(u, c, field, when):
        firsts[u, c] = remote(g.at[u, c, field:field + 2], g.at[u, c, 2:4], d1, when=when, at=xsem.at[u, c, 0])

    def to_second(u, c, field, when):
        seconds[u, c] = remote(g.at[u, c, field:field + 2], g.at[u, c, 4:6], d2, when=when, at=xsem.at[u, c, 1])

    def relay_first(u, c, when):
        remote(g.at[u, c, 2:4], g.at[u, c, 4:6], dev(xx=step(x, -1)), when=when, at=xsem.at[u, c, 1])

    def shift_z(u, c, when):
        behind[u, c] = remote(g.at[u, c, 0:2], g.at[u, c, 6:8], up, when=when)

    def lend(u, c, when):
        lent[u, c] = remote(g.at[u, c, 0:2], g.at[u, c, 6:8], dev(xx=3 - x), when=when)

    def pass_back(u, c):
        pl.when(high)(lent[u, c].wait_recv)
        at = jnp.where(last, 0, 1)
        remote(g.at[u, c, 6:8], g.at[u, c, pl.ds(2 + 2 * at, 2)], dev(xx=3, zz=step(zl, -1)), when=high, at=xsem.at[u, c, at])

    def hand_on(u, c, when):
        pl.when(when)(firsts[u, c].wait_recv)
        relay_first(u, c, when)

    def bring_on(u, c):
        pl.when(low)(behind[u, c].wait_recv)
        to_first(u, c, 6, x == 0)
        to_second(u, c, 6, low)

    def arrived_first(u, c):
        if c in VIA_LOW:
            if u == 0:
                bring_on(u, c)
            firsts[u, c].wait_recv()
        else:
            pl.when(low)(firsts[u, c].wait_recv)

    def spread(src, dst, when=None, at=None):
        return [remote(src(step(y, d)), dst, dev(yy=step(y, d)), when=when, at=None if at is None else at(d)) for d in (1, 2, 3)]

    def wait_all(cps):
        for cp in cps:
            cp.wait_recv()

    def select(u, c):
        def body(i, carry):
            at = pl.ds(pl.multiple_of(i * 8, 8), 8)
            for ri in range(2):
                cand = [g[u, c, f, ri, at, :] for f in range(1, 6)]
                for p in range(4):
                    first = p // 2
                    m = of[first, p % 2]
                    v = cand[first + 3]
                    for o in (3, 2, 1):
                        v = jnp.where(m == F32(o), cand[first + o - 1], v)
                    tsel[u, c, p, ri, at, :] = v
            return carry
        lax.fori_loop(0, rows // 8, body, 0)

    t0, cross, s1, t1 = {}, {}, {}, {}
    own_t0, own_s1, own_t1 = [], {}, []
    fs, ft = [], []

    def go_across(c):
        cross[c] = remote(g.at[0, c, 0:2], g.at[1, c, 0:2], across)

    for c in range(NC):
        keep[c].wait()
        sib_g[c].wait_recv()
        if c in VIA_HIGH:
            lend(0, c, low)
    for c in range(NC):
        to_first(0, c, 0, x >= 1)
        to_second(0, c, 0, second)
    s0 = spread(lambda yd: g.at[0, :, yd // 2], sl.at[a, y])
    own_s0 = local(g.at[0, :, y // 2], sl.at[a, y])
    for c in VIA_HIGH:
        pass_back(0, c)
        go_across(c)
    go_across(1)
    for c in VIA_LOW:
        shift_z(0, c, low)
        if c > 1:
            go_across(c)
    for c in VIA_HIGH:
        hand_on(0, c, high)
    for c in VIA_LOW:
        to_second(0, c, 0, last)
    sib_of.wait_recv()

    def crossed(c):
        cross[c].wait_recv()
        to_first(1, c, 0, x >= 1)
        to_second(1, c, 0, high if c in VIA_LOW else second)
        if c in VIA_LOW:
            shift_z(1, c, low)
        else:
            lend(1, c, low)
        s1[c] = spread(lambda yd: g.at[1, c, yd // 2], sb.at[y, c])
        own_s1[c] = local(g.at[1, c, y // 2], sb.at[y, c])

    for c in range(NC):
        arrived_first(0, c)
        seconds[0, c].wait_recv()
        select(0, c)
        t0[c] = spread(lambda yd: tsel.at[0, c, yd], tl.at[a, y, c])
        own_t0.append(local(tsel.at[0, c, y], tl.at[a, y, c]))
        crossed(c)
        if c >= 1:
            pass_back(1, c - 1) if c - 1 in VIA_HIGH else None
        if c >= 2 and c - 2 in VIA_HIGH:
            hand_on(1, c - 2, second)
    for c in VIA_HIGH:
        hand_on(1, c, last)

    def forward(dst, index):
        return remote(dst.at[a, index], dst.at[a, index], sib)

    own_s0.wait()
    fs.append(forward(sl, y))
    for d in (1, 2, 3):
        s0[d - 1].wait_recv()
        fs.append(forward(sl, step(y, -d)))

    def prepare_left(src, dst, ch, yi):
        at = pl.ds(pl.multiple_of(yi * rows, rows), rows)
        for ri in range(2):
            for c in range(NC):
                hi, lo = split(src[ch, yi, c, ri])
                cols = slice((2 * c + ri) * wide, (2 * c + ri + 1) * wide)
                dst[0, ch, at, cols] = hi
                dst[1, ch, at, cols] = lo

    def prepare_right(src, dst, yi, c):
        at0 = pl.ds(pl.multiple_of(yi * 2 * rows, rows), rows)
        at1 = pl.ds(pl.multiple_of(yi * 2 * rows + rows, rows), rows)
        rh, rl = split(src[yi, c, 0])
        ih, il = split(src[yi, c, 1])
        for n, re, im in ((0, rh, ih), (1, rl, il)):
            dst[n, c, at0, 0:wide] = re
            dst[n, c, at0, wide:2 * wide] = im
            dst[n, c, at1, 0:wide] = -im
            dst[n, c, at1, wide:2 * wide] = re

    def multiply(left, ch, right, acc, fresh, first, last):
        def body(c, carry):
            lh = left[0, ch]
            rh = right[0, c]
            r = jnp.dot(lh, rh, preferred_element_type=F32)
            r += jnp.dot(lh, right[1, c], preferred_element_type=F32)
            r += jnp.dot(left[1, ch], rh, preferred_element_type=F32)
            for ri in range(2):
                v = r[:, ri * wide:(ri + 1) * wide]
                acc[c, ri] = v if fresh else acc[c, ri] + v
            return carry
        lax.fori_loop(first, last, body, 0)

    def loop(n, fn):
        def body(i, carry):
            fn(i)
            return carry
        lax.fori_loop(0, n, body, 0)

    def prep_s(i):
        prepare_left(sl, ls, 0, i)
        prepare_left(sl, ls, 1, i)

    def prep_t(i):
        prepare_left(tl, lt, 0, i)
        prepare_left(tl, lt, 1, i)

    for cp in own_t0:
        cp.wait()
    ft.append(forward(tl, y))
    for d in (1, 2, 3):
        for cc in range(NC):
            t0[cc][d - 1].wait_recv()
        ft.append(forward(tl, step(y, -d)))

    def prep_left():
        loop(4, prep_s)
        loop(4, prep_t)
        loop(16, lambda i: prepare_right(sl.at[a], rs, i // NC, i % NC))
        loop(16, lambda i: prepare_right(tl.at[a], rt, i // NC, i % NC))

    wait_all(fs)
    wait_all(ft)

    for c in VIA_LOW:
        bring_on(1, c)

    @pl.when(x >= 1)
    def _():
        prep_left()
        multiply(ls, h, rt, pacc, True, 0, NC)
        multiply(lt, h, rs, qacc, True, 0, NC)

    for c in range(NC):
        arrived_first(1, c)
        seconds[1, c].wait_recv()
        select(1, c)
        t1[c] = spread(lambda yd: tsel.at[1, c, yd], tb.at[y, c])
        own_t1.append(local(tsel.at[1, c, y], tb.at[y, c]))
        if c == 1:
            pl.when(x == 0)(prep_left)
        if c == 2:
            pl.when(x == 0)(lambda: multiply(ls, h, rt, pacc, True, 0, NC))
        if c == 3:
            pl.when(x == 0)(lambda: multiply(lt, h, rs, qacc, True, 0, NC))

    def cross_rows_of_q():
        for c in range(NC):
            own_s1[c].wait()
            wait_all(s1[c])
        loop(16, lambda i: prepare_right(sb, rs, i // NC, i % NC))
        multiply(lt, 1 - h, rs, qacc, False, 0, NC)

    src_core = y // 2
    k = y % 2
    home = src_core == a
    away = src_core != a
    back = []
    for c in range(NC):
        if c == 2:
            cross_rows_of_q()
        own_t1[c].wait()
        wait_all(t1[c])
        loop(4, lambda i: prepare_right(tb, rt, i, c))
        multiply(ls, 1 - h, rt, pacc, False, c, c + 1)
        for d in (1, 2, 3, 0):
            yd = step(y, d)
            src = pacc.at[c, :, pl.ds(pl.multiple_of(yd * rows, rows), rows), :]
            dst = out.at[k, :, :, columns(a, c)]
            if d == 0:
                lcp = pltpu.make_async_copy(src, dst, lsem.at[20 + c])
                pl.when(home)(lcp.start)
                back.append(lcp)
                remote(src, dst, sib, when=away, at=psem.at[k, a, c])
            else:
                remote(src, dst, dev(core=src_core, yy=yd), at=psem.at[k, a, c])


    def tr_body(i, acc):
        c = i // (4 * rows // 16)
        at = pl.ds(pl.multiple_of((i % (4 * rows // 16)) * 16, 16), 16)
        for ri in range(2):
            v = pacc[c, ri, at, :] * qacc[c, ri, at, :]
            acc = acc + v
        return acc
    total = lax.fori_loop(0, NC * 4 * rows // 16, tr_body, jnp.zeros((16, wide), F32))
    total = total[0:8] + total[8:16]

    part[...] = total
    slot = 2 * h + a
    for dh in (1, 0):
        for d in (1, 2, 3, 0):
            dst = parts.at[k, slot]
            if d == 0 and dh == 0:
                @pl.when(home)
                def _():
                    parts[k, slot] = part[...]
                remote(part, dst, sib, when=away, at=trsem.at[k, slot])
            else:
                remote(part, dst, dev(core=src_core, yy=step(y, d), hh=(h + dh) % 2), at=trsem.at[k, slot])

    def expect(dst, sem, unless):
        cp = pltpu.make_async_remote_copy(src_ref=dst, dst_ref=dst, send_sem=ssem.at[0], recv_sem=sem, device_id=sib, device_id_type=MESH)
        pl.when(jnp.logical_not(unless))(cp.wait_recv)

    for kk in range(2):
        for ch in range(2):
            for hh in range(2):
                expect(parts.at[kk, 2 * hh + ch], trsem.at[kk, 2 * hh + ch], (y == 2 * a + kk) & (ch == a) & (hh == h))
    width = F32(8 * rows)
    for kk in range(2):
        trace = parts[kk, 0] + parts[kk, 1] + parts[kk, 2] + parts[kk, 3]
        corr[0, kk] = jnp.sum(trace) / width

    for kk in range(2):
        for ch in range(2):
            for c in range(NC):
                expect(out.at[kk, :, :, columns(ch, c)], psem.at[kk, ch, c], (y == 2 * a + kk) & (ch == a))
    for lcp in back:
        pl.when(home)(lcp.wait)
    for cp, when in sends:
        if when is None:
            cp.wait_send()
        else:
            pl.when(when)(cp.wait_send)


def body(fields, offsets):
    own = fields[0]
    rows, width = own.shape[1], own.shape[2]
    half = width // 2
    block = (2, rows, 128)
    out, corr = pl.pallas_call(
        functools.partial(kernel, rows),
        out_shape=(jax.ShapeDtypeStruct((2, 2, rows, width), F32), jax.ShapeDtypeStruct((1, 2), F32)),
        in_specs=[pl.BlockSpec(memory_space=pl.ANY), pl.BlockSpec(memory_space=pltpu.SMEM)],
        out_specs=(pl.BlockSpec(memory_space=pl.ANY), pl.BlockSpec(memory_space=pltpu.SMEM)),
        scratch_shapes=[
            pltpu.VMEM((2, NC, 8) + block, F32),
            pltpu.VMEM((2, 2, 8, 128), F32),
            pltpu.VMEM((2, NC, 4) + block, F32),
            pltpu.VMEM((2, 4, NC) + block, F32),
            pltpu.VMEM((2, 4, NC) + block, F32),
            pltpu.VMEM((4, NC) + block, F32),
            pltpu.VMEM((4, NC) + block, F32),
            pltpu.VMEM((2, 2, half, width), BF16),
            pltpu.VMEM((2, 2, half, width), BF16),
            pltpu.VMEM((2, NC, width, 256), BF16),
            pltpu.VMEM((2, NC, width, 256), BF16),
            pltpu.VMEM((NC, 2, half, 128), F32),
            pltpu.VMEM((NC, 2, half, 128), F32),
            pltpu.VMEM((8, 128), F32),
            pltpu.VMEM((2, 4, 8, 128), F32),
            pltpu.SemaphoreType.DMA((NSEM,)),
            pltpu.SemaphoreType.DMA((NSEM,)),
            pltpu.SemaphoreType.DMA((NC, 3)),
            pltpu.SemaphoreType.DMA((2, NC, 2)),
            pltpu.SemaphoreType.DMA((2, 2, NC)),
            pltpu.SemaphoreType.DMA((2, 4)),
            pltpu.SemaphoreType.DMA((24,)),
        ],
        compiler_params=pltpu.CompilerParams(collective_id=0, has_side_effects=True, vmem_limit_bytes=60 * 2**20),
        cost_estimate=pl.CostEstimate(flops=13 * 10**9, bytes_accessed=4 * 2**20, transcendentals=0),
        name="contract",
    )(own, offsets)
    return out[None], corr


def solution(mesh):
    in_specs = (P("tm", None, "mode", None), P("tm", None))
    out_specs = (P("tm", None, None, "mode", None), P("tm", None))
    return jax.shard_map(body, mesh=mesh, in_specs=in_specs, out_specs=out_specs, check_vma=False)
```
